128 devices in a mesh: gx: 8 (over z, core), gy: 16 (over y, x).
Axes of the slice: x: 4, y: 4, z: 4, core: 2. Of those that a mesh axis runs over, the one named last changes fastest.
Arguments:
- features: bfloat16 [131072, 512], P(('gx', 'gy')), may hold values from -6 to 6
- coefficients: bfloat16 [2048, 64, 512], P(('gx', 'gy')), may hold values from -0.25 to 0.25
- source_blocks: int32 [2048, 8], P(('gx', 'gy')), may hold values from 0 to 21, as said below
- send_x: int32 [128, 2, 1], P(('gx', 'gy')), may hold values from 0 to 15
- send_y: int32 [128, 2, 2], P(('gx', 'gy')), may hold values from 0 to 15
- node_counts: int32 [128], P(('gx', 'gy')), may hold values from 256 to 1024, as said below
- w_msg_in: bfloat16 [2, 512, 512], replicated, may hold values from -0.25 to 0.25
- w_msg_out: bfloat16 [2, 512, 512], replicated, may hold values from -0.25 to 0.25
- w_node_in: bfloat16 [2, 1024, 512], replicated, may hold values from -0.1875 to 0.1875
- b_node: float32 [2, 512], replicated, may hold values from -3 to 3
- w_node_out: bfloat16 [2, 512, 512], replicated, may hold values from -0.25 to 0.25
- ln_gain: float32 [2, 512], replicated, may hold values from 0.1 to 1.9
Outputs:
- latents: bfloat16 [131072, 512], P(('gx', 'gy'))
The draws below stay inside these ranges and needn't reach their ends.
Inputs may be any that keep to these rules, and one draw needn't show every extreme that they name: `node_counts`: A partition's live nodes are its first slots; some partition is full and some holds a quarter of 1024. `source_blocks`: indices below 16 name local blocks, then 1 block from the lower and 1 from the upper first-direction neighbour, then 2 and 2 of the second direction; slots 0 to 5 of every block name local blocks, the last two slots name blocks received from neighbours. `send_x`: local block indices, repeats allowed. `send_y`: local block indices, repeats allowed.
All inputs are finite; a program needn't handle non-finite values.
Results may differ from the reference program's by a relative error of at most 0.013.
Values may be sent and summed in bfloat16 or wider, within the bound.
A program may use at most 64 MiB of HBM per device.

```python
import jax
import jax.numpy as jnp
from jax import lax

H = 512
BS = 64
K = 8
NBD = 16
LAYERS = 2
HX = 1
HY = 2
POOL = 22
NODE_DEV = 1024
PARTS_SIZE = 128
NBLOCKS = 2048
NODES = 131072
N_GX = 8
N_GY = 16


def draw_node_counts(key, part):
    key = jax.random.fold_in(key, 7)
    key_base, key_full, key_small = jax.random.split(key, 3)
    counts_drawn = jax.random.randint(key_base, (PARTS_SIZE,), NODE_DEV // 4, NODE_DEV + 1)
    full_part = jax.random.randint(key_full, (), 0, PARTS_SIZE)
    small_part = (full_part + 1 + jax.random.randint(key_small, (), 0, PARTS_SIZE - 1)) % PARTS_SIZE
    positions = jnp.arange(PARTS_SIZE)
    counts_drawn = jnp.where(positions == full_part, NODE_DEV, counts_drawn)
    counts_drawn = jnp.where(positions == small_part, NODE_DEV // 4, counts_drawn)
    return counts_drawn.astype(jnp.int32)


def draw_source_blocks(key, part):
    key = jax.random.fold_in(key, 11)
    key_local, key_halo = jax.random.split(key, 2)
    local_slots = jax.random.randint(key_local, (NBLOCKS, K - 2), 0, NBD)
    halo_slots = jax.random.randint(key_halo, (NBLOCKS, 2), NBD, NBD + 2 * HX + 2 * HY)
    return jnp.concatenate([local_slots, halo_slots], 1).astype(jnp.int32)


def plant(array, own_key, least, top_value):
    spot = [jax.random.randint(jax.random.fold_in(own_key, axis), (), 0, length) for axis, length in enumerate(array.shape)]
    widest = array.shape.index(max(array.shape))
    neighbour = spot[:widest] + [(spot[widest] + 1) % array.shape[widest]] + spot[widest + 1:]
    return array.at[tuple(spot)].set(least).at[tuple(neighbour)].set(top_value)


def levels(own_key, extent, cuts, least, largest):
    loudness = 1.0
    for dim, shards_of in cuts:
        draws = jax.random.uniform(jax.random.fold_in(jax.random.fold_in(own_key, 6), dim), (shards_of,), jnp.float32, least / len(cuts), largest / len(cuts))
        loudness = loudness * jnp.repeat(jnp.exp(draws), extent[dim] // shards_of).reshape((-1,) + (1,) * (len(extent) - 1 - dim))
    return loudness


def normal_values(rng, dims, width, most, cuts=(), kind=jnp.bfloat16):
    level = levels(rng, dims, cuts, -0.22, 0.18) if cuts else 1.0
    array = jax.random.normal(rng, dims, jnp.float32) * width * level
    return jnp.minimum(jnp.maximum(array, -most), most).astype(kind)


def setup_inputs(seed: int = 0) -> dict:
    key_of = jax.random.split(jax.random.key(seed), 13)
    return {
        "features": normal_values(key_of[0], (NODES, H), 1.0, 6.0, ((0, 128),)),
        "coefficients": normal_values(key_of[1], (NBLOCKS, BS, K * BS), (K * BS) ** -0.5, 0.25, ((0, 128),)),
        "source_blocks": draw_source_blocks(jax.random.fold_in(key_of[12], 71), 0),
        "send_x": plant(jax.random.randint(key_of[3], (PARTS_SIZE, 2, HX), 0, NBD), jax.random.fold_in(key_of[3], 1), 0, NBD - 1).astype(jnp.int32),
        "send_y": plant(jax.random.randint(key_of[4], (PARTS_SIZE, 2, HY), 0, NBD), jax.random.fold_in(key_of[4], 1), 0, NBD - 1).astype(jnp.int32),
        "node_counts": draw_node_counts(jax.random.fold_in(key_of[12], 71), 0),
        "w_msg_in": normal_values(key_of[6], (LAYERS, H, H), H ** -0.5, 0.25),
        "w_msg_out": normal_values(key_of[7], (LAYERS, H, H), H ** -0.5, 0.25),
        "w_node_in": normal_values(key_of[8], (LAYERS, 2 * H, H), (2 * H) ** -0.5, 0.1875),
        "b_node": normal_values(key_of[9], (LAYERS, H), 0.5, 3.0, (), jnp.float32),
        "w_node_out": normal_values(key_of[10], (LAYERS, H, H), H ** -0.5, 0.25),
        "ln_gain": jnp.clip(1.0 + 0.18 * jax.random.normal(key_of[11], (LAYERS, H), jnp.float32), 0.1, 1.9),
    }


def message_mlp(states, weight_in, weight_out):
    hidden = jax.nn.silu(jnp.dot(states, weight_in, preferred_element_type=jnp.float32)).astype(jnp.bfloat16)
    return jnp.dot(hidden, weight_out, preferred_element_type=jnp.float32).astype(jnp.bfloat16)

def node_update(source_pool, sources, coeff_block, states, live, node_in, node_bias, node_out, gain):
    gathered = source_pool[sources].reshape(NBD, K * BS, H)
    aggregate = jnp.einsum('brc,bch->brh', coeff_block.astype(jnp.float32), gathered.astype(jnp.float32))
    aggregate = aggregate.astype(jnp.bfloat16).reshape(NODE_DEV, H)
    pre_act = jnp.dot(states, node_in[:H], preferred_element_type=jnp.float32)
    pre_act = pre_act + jnp.dot(aggregate, node_in[H:], preferred_element_type=jnp.float32) + node_bias
    node_hidden = jax.nn.silu(pre_act).astype(jnp.bfloat16)
    update_raw = jnp.dot(node_hidden, node_out, preferred_element_type=jnp.float32)
    row_mean = lax.optimization_barrier(jnp.mean(update_raw, axis=1, keepdims=True))
    row_var = lax.optimization_barrier(jnp.mean((update_raw - row_mean) ** 2, axis=1, keepdims=True))
    normed = (update_raw - row_mean) * lax.rsqrt(row_var + 1e-05)
    return ((states.astype(jnp.float32) + gain * normed) * live).astype(jnp.bfloat16)

def select_blocks(messages, lists):
    return jax.vmap(jax.vmap(lambda m, s: m[s]))(messages, lists)

def reference(features, coefficients, source_blocks, send_x, send_y, node_counts, w_msg_in, w_msg_out, w_node_in, b_node, w_node_out, ln_gain):
    positions = jnp.arange(NODE_DEV, dtype=jnp.int32)
    live = (positions[None, :] < node_counts[:, None]).astype(jnp.float32).reshape(NODES, 1)
    states = (features.astype(jnp.float32) * live).astype(jnp.bfloat16)
    sends_x = send_x.reshape(N_GX, N_GY, 2, HX)
    sends_y = send_y.reshape(N_GX, N_GY, 2, HY)
    sources = source_blocks.reshape(PARTS_SIZE, NBD, K)
    coeff_parts = coefficients.reshape(PARTS_SIZE, NBD, BS, K * BS)
    live_parts = live.reshape(PARTS_SIZE, NODE_DEV, 1)
    for layer_index in range(LAYERS):
        messages = message_mlp(states, w_msg_in[layer_index], w_msg_out[layer_index]).reshape(N_GX, N_GY, NBD, BS, H)
        to_upper_x = select_blocks(messages, sends_x[:, :, 0])
        to_lower_x = select_blocks(messages, sends_x[:, :, 1])
        to_upper_y = select_blocks(messages, sends_y[:, :, 0])
        to_lower_y = select_blocks(messages, sends_y[:, :, 1])
        lower_x = jnp.concatenate([jnp.zeros_like(to_upper_x[:1]), to_upper_x[:-1]], 0)
        upper_x = jnp.concatenate([to_lower_x[1:], jnp.zeros_like(to_lower_x[:1])], 0)
        lower_y = jnp.concatenate([jnp.zeros_like(to_upper_y[:, :1]), to_upper_y[:, :-1]], 1)
        upper_y = jnp.concatenate([to_lower_y[:, 1:], jnp.zeros_like(to_lower_y[:, :1])], 1)
        source_pool = jnp.concatenate([messages, lower_x, upper_x, lower_y, upper_y], 2).reshape(PARTS_SIZE, POOL, BS, H)
        state_parts = states.reshape(PARTS_SIZE, NODE_DEV, H)

        def one_part(items, layer_index=layer_index):
            return node_update(items[0], items[1], items[2], items[3], items[4], w_node_in[layer_index], b_node[layer_index], w_node_out[layer_index], ln_gain[layer_index])
        states = lax.map(one_part, (source_pool, sources, coeff_parts, state_parts, live_parts)).reshape(NODES, H)
    return states
```

```python
import functools

import jax
import jax.numpy as jnp
from jax import lax
from jax.experimental import pallas as pl
from jax.experimental.pallas import tpu as pltpu
from jax.sharding import PartitionSpec as P

MESH = pl.DeviceIdType.MESH
F32 = jnp.float32
BF16 = jnp.bfloat16


def dot(left, right):
    return jnp.dot(left, right, preferred_element_type=F32)


def silu(value):
    return value * jax.nn.sigmoid(value)


def plan(sources_in, send_x, send_y, pos, perm, sources, listed):
    slots, blocks = sources_in.shape
    sent = [send_x[0, 0, 0], send_x[0, 0, 1]] + [send_y[0, side, n] for side in (0, 1) for n in (0, 1)]
    is_sent = []
    for block in range(blocks):
        hit = sent[0] == block
        for other in sent[1:]:
            hit = jnp.logical_or(hit, other == block)
        is_sent.append(hit.astype(jnp.int32))
    total = functools.reduce(lambda a, b: a + b, is_sent)
    first, rest = jnp.int32(0), total
    places = []
    for block in range(blocks):
        place = jnp.where(is_sent[block] == 1, first, rest)
        first = first + is_sent[block]
        rest = rest + 1 - is_sent[block]
        pos[block] = place
        places.append(place)
    for place in range(blocks):
        owner = jnp.int32(0)
        for block in range(1, blocks):
            owner = jnp.where(places[block] == place, block, owner)
        perm[place] = owner
    for n in range(len(sent)):
        listed[n] = pos[sent[n]]
    for block in range(blocks):
        for slot in range(slots - 2):
            sources[block, slot] = pos[sources_in[slot, block]]
        for slot in range(slots - 2, slots):
            sources[block, slot] = jnp.maximum(sources_in[slot, block] - blocks, 0)


def kernel(
    sources_in, send_x, send_y, counts, b_node, ln_gain,
    features, coefficients, w_msg_in, w_msg_out, w_node_in, w_node_out,
    out,
    pos, perm, sources, listed,
    feat, coef, w_mi, w_mo, w_ni, w_no, merged, states, hid, sent, halo_first, halo_second, pre, agg,
    load_sem, send_sem, recv_sem,
):
    blocks, size, width = feat.shape
    n_sent = sent.shape[1]
    halo = (halo_first, halo_second)
    near = (coef.shape[2] // size - 2) * size
    i, j = lax.axis_index("gx"), lax.axis_index("gy")
    n_i, n_j = lax.axis_size("gx"), lax.axis_size("gy")
    up_x, low_x = lax.rem(i + 1, n_i), lax.rem(i + n_i - 1, n_i)
    up_y, low_y = lax.rem(j + 1, n_j), lax.rem(j + n_j - 1, n_j)

    loads = {}

    def load(name, source, target):
        copy = pltpu.make_async_copy(source, target, load_sem.at[len(loads)])
        copy.start()
        loads[name] = copy

    load("feat", features, feat)
    load("mi0", w_msg_in.at[0], w_mi.at[0])
    load("mo0", w_msg_out.at[0], w_mo.at[0])
    load("ni0", w_node_in.at[0], w_ni.at[0])
    load("coef", coefficients, coef)
    load("no0", w_node_out.at[0], w_no.at[0])
    load("mi1", w_msg_in.at[1], w_mi.at[1])
    load("mo1", w_msg_out.at[1], w_mo.at[1])
    load("ni1", w_node_in.at[1], w_ni.at[1])
    load("no1", w_node_out.at[1], w_no.at[1])

    neighbours = [(up_x, j), (low_x, j), (i, up_y), (i, low_y)]
    barrier = pltpu.get_barrier_semaphore()
    for neighbour in neighbours:
        pl.semaphore_signal(barrier, inc=1, device_id=neighbour, device_id_type=MESH)

    plan(sources_in, send_x, send_y, pos, perm, sources, listed)
    count = counts[0, 0]
    row = lax.broadcasted_iota(jnp.int32, (size, 1), 0)

    def live(block):
        return row + block * size < count

    def transfers(layer):
        spans = [(0, 1, neighbours[0]), (1, 2, neighbours[1]), (2, 4, neighbours[2]), (4, 6, neighbours[3])]
        return [
            pltpu.make_async_remote_copy(
                src_ref=sent.at[layer, lo:hi],
                dst_ref=halo[layer].at[lo:hi],
                send_sem=send_sem.at[layer, n],
                recv_sem=recv_sem.at[layer, n],
                device_id=neighbour,
                device_id_type=MESH,
            )
            for n, (lo, hi, neighbour) in enumerate(spans)
        ]

    def fill_states(lo, hi):
        for place in range(lo, hi):
            block = perm[place]
            states[0, place] = jnp.where(live(block), feat[block], jnp.zeros((), BF16))

    def hidden(layer, lo, hi):
        rows = states[layer, lo:hi].reshape((hi - lo) * size, width)
        hid[layer, lo:hi] = silu(dot(rows, w_mi[layer])).astype(BF16).reshape(hi - lo, size, width)

    def fill_sent(layer):
        for n in range(n_sent):
            sent[layer, n] = hid[layer, listed[n]]

    def merge(layer):
        merged[layer] = dot(w_mo[layer], w_ni[layer, width:]).astype(BF16)

    def pre_states(layer):
        rows = states[layer].reshape(blocks * size, width)
        pre[...] = (dot(rows, w_ni[layer, :width]) + b_node[layer][None, :]).reshape(blocks, size, width)

    def own_part(layer, at):
        for place in range(blocks):
            block = at(place)
            picked = jnp.concatenate([hid[layer, sources[block, slot]] for slot in range(near // size)], 0)
            agg[place] = dot(coef[block, :, :near], picked)

    def exists(source):
        low_i, high_i = (i > 0).astype(jnp.int32), (i < n_i - 1).astype(jnp.int32)
        low_j, high_j = (j > 0).astype(jnp.int32), (j < n_j - 1).astype(jnp.int32)
        return jnp.where(source == 0, low_i, jnp.where(source == 1, high_i, jnp.where(source < 4, low_j, high_j)))

    def whole_aggregate(layer, place, block):
        first, second = sources[block, near // size], sources[block, near // size + 1]
        picked = jnp.concatenate(
            [
                jnp.where(exists(first) == 1, halo[layer][first], jnp.zeros((), BF16)),
                jnp.where(exists(second) == 1, halo[layer][second], jnp.zeros((), BF16)),
            ],
            0,
        )
        return agg[place] + dot(coef[block, :, near:], picked)

    def update(layer, aggregate, base, old, alive):
        node_hidden = silu(base + dot(aggregate.astype(BF16), merged[layer])).astype(BF16)
        raw = dot(node_hidden, w_no[layer])
        centred = raw - jnp.mean(raw, axis=1, keepdims=True)
        variance = jnp.mean(centred * centred, axis=1, keepdims=True)
        normed = centred * lax.rsqrt(variance + 1e-05)
        return jnp.where(alive, old.astype(F32) + ln_gain[layer][None, :] * normed, 0.0).astype(BF16)

    def advance(lo, hi):
        aggregate = jnp.concatenate([whole_aggregate(0, place, perm[place]) for place in range(lo, hi)], 0)
        rows = (hi - lo) * size
        alive = jnp.concatenate([live(perm[place]) for place in range(lo, hi)], 0)
        base, old = pre[lo:hi].reshape(rows, width), states[0, lo:hi].reshape(rows, width)
        states[1, lo:hi] = update(0, aggregate, base, old, alive).reshape(hi - lo, size, width)

    loads["feat"].wait()
    fill_states(0, n_sent)
    loads["mi0"].wait()
    hidden(0, 0, n_sent)
    fill_sent(0)
    pl.semaphore_wait(barrier, len(neighbours))
    first = transfers(0)
    for copy in first:
        copy.start()

    fill_states(n_sent, blocks)
    for name in ("mo0", "ni0", "coef", "mo1", "ni1"):
        loads[name].wait()
    hidden(0, n_sent, blocks)
    merge(0)
    pre_states(0)
    own_part(0, lambda place: perm[place])
    merge(1)
    for name in ("no0", "mi1", "no1"):
        loads[name].wait()

    for copy in first:
        copy.wait_recv()
    for lo in range(0, n_sent, 2):
        advance(lo, lo + 2)
        hidden(1, lo, lo + 2)
    fill_sent(1)
    second = transfers(1)
    for copy in second:
        copy.start()

    for lo in range(n_sent, blocks, 2):
        advance(lo, lo + 2)
    hidden(1, n_sent, blocks)
    pre_states(1)
    own_part(1, lambda place: place)

    for copy in second:
        copy.wait_recv()
    step = 4
    for lo in range(0, blocks, step):
        hi, rows = lo + step, step * size
        aggregate = jnp.concatenate([whole_aggregate(1, block, block) for block in range(lo, hi)], 0)
        base = jnp.concatenate([pre[pos[block]] for block in range(lo, hi)], 0)
        old = jnp.concatenate([states[1, pos[block]] for block in range(lo, hi)], 0)
        alive = jnp.concatenate([live(block) for block in range(lo, hi)], 0)
        out[lo * size : hi * size] = update(1, aggregate, base, old, alive)
    for copy in first + second:
        copy.wait_send()


def body(
    features, coefficients, source_blocks, send_x, send_y, node_counts,
    w_msg_in, w_msg_out, w_node_in, b_node, w_node_out, ln_gain,
):
    blocks, size, fan = coefficients.shape
    nodes, width = features.shape
    layers = w_msg_in.shape[0]
    n_sent = send_x.shape[1] * send_x.shape[2] + send_y.shape[1] * send_y.shape[2]
    smem, vmem, any_ = (pl.BlockSpec(memory_space=space) for space in (pltpu.SMEM, pltpu.VMEM, pltpu.HBM))
    return pl.pallas_call(
        kernel,
        out_shape=jax.ShapeDtypeStruct((nodes, width), BF16),
        in_specs=[smem] * 4 + [vmem] * 2 + [any_] * 6,
        out_specs=vmem,
        scratch_shapes=[
            pltpu.SMEM((blocks,), jnp.int32),
            pltpu.SMEM((blocks,), jnp.int32),
            pltpu.SMEM(source_blocks.shape, jnp.int32),
            pltpu.SMEM((n_sent,), jnp.int32),
            pltpu.VMEM((blocks, size, width), BF16),
            pltpu.VMEM((blocks, size, fan), BF16),
            pltpu.VMEM(w_msg_in.shape, BF16),
            pltpu.VMEM(w_msg_out.shape, BF16),
            pltpu.VMEM(w_node_in.shape, BF16),
            pltpu.VMEM(w_node_out.shape, BF16),
            pltpu.VMEM(w_msg_out.shape, BF16),
            pltpu.VMEM((layers, blocks, size, width), BF16),
            pltpu.VMEM((layers, blocks, size, width), BF16),
            pltpu.VMEM((layers, n_sent, size, width), BF16),
            pltpu.VMEM((n_sent, size, width), BF16),
            pltpu.VMEM((n_sent, size, width), BF16),
            pltpu.VMEM((blocks, size, width), F32),
            pltpu.VMEM((blocks, size, width), F32),
            pltpu.SemaphoreType.DMA((10,)),
            pltpu.SemaphoreType.DMA((layers, 4)),
            pltpu.SemaphoreType.DMA((layers, 4)),
        ],
        compiler_params=pltpu.CompilerParams(
            collective_id=0, has_side_effects=True, vmem_limit_bytes=62 * 2**20
        ),
        cost_estimate=pl.CostEstimate(flops=6 * 10**9, bytes_accessed=9 * 2**20, transcendentals=2 * 10**6),
    )(
        source_blocks.T, send_x.transpose(0, 2, 1), send_y, node_counts.reshape(1, 1), b_node, ln_gain,
        features.reshape(blocks, size, width), coefficients, w_msg_in, w_msg_out, w_node_in, w_node_out,
    )


def solution(mesh):
    split = ("gx", "gy")
    return jax.shard_map(
        body,
        mesh=mesh,
        in_specs=(
            P(split, None), P(split, None, None), P(split, None), P(split, None, None), P(split, None, None),
            P(split), P(), P(), P(), P(), P(), P(),
        ),
        out_specs=P(split, None),
        check_vma=False,
    )
```

```python
import functools

import jax
import jax.numpy as jnp
from jax import lax
from jax.experimental import pallas as pl
from jax.experimental.pallas import tpu as pltpu
from jax.sharding import PartitionSpec as P

MESH = pl.DeviceIdType.MESH
F32 = jnp.float32
BF16 = jnp.bfloat16
FAR = 2


def dot(left, right):
    return jnp.dot(left, right, preferred_element_type=F32)


def silu(value):
    return value * jax.nn.sigmoid(value)


def normalised(raw):
    centred = raw - jnp.mean(raw, axis=1, keepdims=True)
    variance = jnp.mean(centred * centred, axis=1, keepdims=True)
    return centred * lax.rsqrt(variance + 1e-05)


def exchange_kernel(
    sources_in, send_x_in, send_y_in, counts, b_node_in, ln_gain_in,
    features, coefficients, w_msg_in, w_msg_out, w_node_in, w_node_out,
    last_hidden, last_states, last_w, last_row,
    sources, send_x, send_y, b_node, ln_gain,
    feat, coef, w_mi, w_mo, w_ni, w_no, merged, states, own, first_states, sent, halo_first, halo_second, base,
    small_sem, load_sem, send_sem, recv_sem,
):
    blocks, size, width = feat.shape
    n_sent = sent.shape[1]
    n_y = send_y.shape[1] * send_y.shape[2]
    near = sources.shape[0] - FAR
    halo = (halo_first, halo_second)
    i, j = lax.axis_index("gx"), lax.axis_index("gy")
    n_i, n_j = lax.axis_size("gx"), lax.axis_size("gy")

    smalls = [
        pltpu.make_async_copy(source, target, small_sem.at[n])
        for n, (source, target) in enumerate(
            [
                (sources_in, sources), (send_x_in, send_x), (send_y_in, send_y),
                (b_node_in, b_node), (ln_gain_in, ln_gain),
            ]
        )
    ]
    pairs = {
        "feat": (features, feat),
        "mi0": (w_msg_in.at[0], w_mi.at[0]),
        "mo0": (w_msg_out.at[0], w_mo.at[0]),
        "ni0": (w_node_in.at[0], w_ni.at[0]),
        "coef": (coefficients, coef),
        "no0": (w_node_out.at[0], w_no.at[0]),
        "mi1": (w_msg_in.at[1], w_mi.at[1]),
        "mo1": (w_msg_out.at[1], w_mo.at[1]),
        "ni1": (w_node_in.at[1], w_ni.at[1]),
        "no1": (w_node_out.at[1], last_w),
    }
    loads = {
        name: pltpu.make_async_copy(source, target, load_sem.at[n]) for n, (name, (source, target)) in enumerate(pairs.items())
    }
    loads["feat"].start()
    for copy in smalls:
        copy.start()
    for name in ("mi0", "mo0", "ni0"):
        loads[name].start()

    lower_x, upper_x = i > 0, i < n_i - 1
    lower_y, upper_y = j > 0, j < n_j - 1
    routes = [
        ((i, jnp.minimum(j + 1, n_j - 1)), upper_y, lower_y, 0, 2),
        ((i, jnp.maximum(j - 1, 0)), lower_y, upper_y, 2, 4),
        ((jnp.minimum(i + 1, n_i - 1), j), upper_x, lower_x, 4, 5),
        ((jnp.maximum(i - 1, 0), j), lower_x, upper_x, 5, 6),
    ]
    barrier = pltpu.get_barrier_semaphore()
    for device, there, _, _, _ in routes:

        @pl.when(there)
        def _():
            pl.semaphore_signal(barrier, inc=1, device_id=device, device_id_type=MESH)

    for _, _, comes, lo, hi in routes:

        @pl.when(jnp.logical_not(comes))
        def _():
            for buffer in halo:
                buffer[lo:hi] = jnp.zeros((hi - lo, size, width), BF16)

    def transfer(layer, n):
        device, there, comes, lo, hi = routes[n]
        copy = pltpu.make_async_remote_copy(
            src_ref=sent.at[layer, lo:hi],
            dst_ref=halo[layer].at[lo:hi],
            send_sem=send_sem.at[layer, n],
            recv_sem=recv_sem.at[layer, n],
            device_id=device,
            device_id_type=MESH,
        )
        return copy, there, comes

    def start(layer, routes_now):
        for n in routes_now:
            copy, there, _ = transfer(layer, n)
            pl.when(there)(copy.start)

    def receive(layer):
        for n in range(len(routes)):
            copy, _, comes = transfer(layer, n)
            pl.when(comes)(copy.wait_recv)

    def drain(layer):
        for n in range(len(routes)):
            copy, there, _ = transfer(layer, n)
            pl.when(there)(copy.wait_send)

    for copy in smalls:
        copy.wait()
    listed = [send_y[0, side, n] for side in (0, 1) for n in range(2)] + [send_x[0, 0, 0], send_x[0, 0, 1]]
    count = counts[0, 0]
    row = lax.broadcasted_iota(jnp.int32, (size, 1), 0)
    zero = jnp.zeros((), BF16)

    def live(block):
        return row + block * size < count

    def stacked(parts):
        return jnp.concatenate(parts, 0)

    def split(rows):
        return rows.reshape(rows.shape[0] // size, size, width)

    def outgoing(layer, rows):
        return dot(silu(dot(rows, w_mi[layer])).astype(BF16), merged[layer]).astype(BF16)

    def merge(layer):
        merged[layer] = dot(w_mo[layer], w_ni[layer, width:]).astype(BF16)

    def own_base(layer, rows_of):
        for lo in range(0, blocks, 4):
            rows = rows_of(lo, lo + 4)
            base[lo : lo + 4] = split(dot(rows, w_ni[layer, :width]) + b_node[layer][None, :])
        for block in range(blocks):
            picked = stacked([own[layer, sources[slot, block]] for slot in range(near)])
            base[block] += dot(coef[block, :, : near * size], picked)

    def pool_index(slot, block):
        index = sources[slot, block] - blocks
        return jnp.clip(jnp.where(index < 2, index + n_y, index - 2), 0, n_sent - 1)

    def activated(layer, block):
        picked = stacked([halo[layer][pool_index(slot, block)] for slot in range(near, near + FAR)])
        return silu(base[block] + dot(coef[block, :, near * size :], picked)).astype(BF16)

    def advanced(blocks_now, old):
        raw = dot(stacked([activated(0, block) for block in blocks_now]), w_no[0])
        alive = stacked([live(block) for block in blocks_now])
        return jnp.where(alive, old.astype(F32) + ln_gain[0][None, :] * normalised(raw), 0.0).astype(BF16)

    loads["feat"].wait()
    for n in range(n_sent):
        first_states[n] = jnp.where(live(listed[n]), feat[listed[n]], zero)
    for name in ("coef", "no0", "mi1", "mo1", "ni1", "no1"):
        loads[name].start()
    for name in ("mi0", "mo0", "ni0"):
        loads[name].wait()
    merge(0)
    sent[0] = split(outgoing(0, first_states[...].reshape(n_sent * size, width)))
    pl.semaphore_wait(barrier, sum(there.astype(jnp.int32) for _, there, _, _, _ in routes))
    start(0, (0, 1, 2, 3))

    for block in range(blocks):
        states[0, block] = jnp.where(live(block), feat[block], zero)
    for lo in range(0, blocks, 4):
        own[0, lo : lo + 4] = split(outgoing(0, states[0, lo : lo + 4].reshape(4 * size, width)))
    loads["coef"].wait()
    own_base(0, lambda lo, hi: states[0, lo:hi].reshape((hi - lo) * size, width))
    for name in ("no0", "mi1", "mo1", "ni1", "no1"):
        loads[name].wait()
    merge(1)

    receive(0)
    for lo, hi, routes_now in ((0, n_y, (0, 1)), (n_y, n_sent, (2, 3))):
        old = first_states[lo:hi].reshape((hi - lo) * size, width)
        sent[1, lo:hi] = split(outgoing(1, advanced(listed[lo:hi], old)))
        start(1, routes_now)

    for lo in range(0, blocks, 4):
        rows = slice(lo * size, (lo + 4) * size)
        last_states[rows] = advanced(range(lo, lo + 4), states[0, lo : lo + 4].reshape(4 * size, width))
    for lo in range(0, blocks, 4):
        own[1, lo : lo + 4] = split(outgoing(1, last_states[lo * size : (lo + 4) * size]))
    own_base(1, lambda lo, hi: last_states[lo * size : hi * size])
    last_row[0:1] = ln_gain[1:2]
    last_row[1:2] = jnp.full((1, width), count, jnp.int32).astype(F32)

    receive(1)
    for block in range(blocks):
        last_hidden[block * size : (block + 1) * size] = activated(1, block)
    drain(0)
    drain(1)


def last_kernel(last_hidden, last_states, last_w, last_row, out, latents, out_sem):
    nodes = last_states.shape[0]
    parts = out_sem.shape[0]
    step = nodes // parts
    gain, count = last_row[0:1], last_row[1:2]
    stores = []
    for n in range(parts):
        rows = slice(n * step, (n + 1) * step)
        normed = normalised(dot(last_hidden[rows], last_w[...]))
        position = lax.broadcasted_iota(jnp.int32, (step, 1), 0) + n * step
        alive = position.astype(F32) < count
        latents[rows] = jnp.where(alive, last_states[rows].astype(F32) + gain * normed, 0.0).astype(BF16)
        store = pltpu.make_async_copy(latents.at[rows], out.at[rows], out_sem.at[n])
        store.start()
        stores.append(store)
    for store in stores:
        store.wait()


def body(
    features, coefficients, source_blocks, send_x, send_y, node_counts,
    w_msg_in, w_msg_out, w_node_in, b_node, w_node_out, ln_gain,
):
    blocks, size, fan = coefficients.shape
    nodes, width = features.shape
    layers = w_msg_in.shape[0]
    n_sent = send_x.shape[1] * send_x.shape[2] + send_y.shape[1] * send_y.shape[2]
    any_, vmem = pl.BlockSpec(memory_space=pl.ANY), pl.BlockSpec(memory_space=pltpu.VMEM)
    operands = [
        source_blocks.T, send_x.transpose(0, 2, 1), send_y, node_counts.reshape(1, 1), b_node, ln_gain,
        features.reshape(blocks, size, width), coefficients, w_msg_in, w_msg_out, w_node_in, w_node_out,
    ]
    operands = [
        operand if operand.size == 1 else pltpu.with_memory_space_constraint(operand, pltpu.HBM) for operand in operands
    ]
    ints = [pltpu.SMEM(operand.shape, jnp.int32) for operand in operands[:3]]
    counted = pl.BlockSpec(memory_space=pltpu.SMEM)
    handed = [((nodes, width), BF16), ((nodes, width), BF16), ((width, width), BF16), ((8, width), F32)]
    between = pl.pallas_call(
        exchange_kernel,
        out_shape=[pltpu.VMEM(shape, dtype) for shape, dtype in handed],
        in_specs=[any_] * 3 + [counted] + [any_] * 8,
        out_specs=[vmem] * len(handed),
        scratch_shapes=ints
        + [
            pltpu.VMEM(b_node.shape, F32),
            pltpu.VMEM(ln_gain.shape, F32),
            pltpu.VMEM((blocks, size, width), BF16),
            pltpu.VMEM((blocks, size, fan), BF16),
            pltpu.VMEM(w_msg_in.shape, BF16),
            pltpu.VMEM(w_msg_out.shape, BF16),
            pltpu.VMEM(w_node_in.shape, BF16),
            pltpu.VMEM((1, width, width), BF16),
            pltpu.VMEM(w_msg_out.shape, BF16),
            pltpu.VMEM((1, blocks, size, width), BF16),
            pltpu.VMEM((layers, blocks, size, width), BF16),
            pltpu.VMEM((n_sent, size, width), BF16),
            pltpu.VMEM((layers, n_sent, size, width), BF16),
            pltpu.VMEM((n_sent, size, width), BF16),
            pltpu.VMEM((n_sent, size, width), BF16),
            pltpu.VMEM((blocks, size, width), F32),
            pltpu.SemaphoreType.DMA((5,)),
            pltpu.SemaphoreType.DMA((10,)),
            pltpu.SemaphoreType.DMA((layers, 4)),
            pltpu.SemaphoreType.DMA((layers, 4)),
        ],
        compiler_params=pltpu.CompilerParams(
            collective_id=0, has_side_effects=True, vmem_limit_bytes=40 * 2**20
        ),
        cost_estimate=pl.CostEstimate(flops=6 * 10**9, bytes_accessed=9 * 2**20, transcendentals=2 * 10**6),
        name="exchange",
    )(*operands)
    return pl.pallas_call(
        last_kernel,
        out_shape=jax.ShapeDtypeStruct((nodes, width), BF16),
        in_specs=[vmem] * len(handed),
        out_specs=any_,
        scratch_shapes=[pltpu.VMEM((nodes, width), BF16), pltpu.SemaphoreType.DMA((4,))],
        compiler_params=pltpu.CompilerParams(vmem_limit_bytes=40 * 2**20),
        cost_estimate=pl.CostEstimate(flops=6 * 10**8, bytes_accessed=2**20, transcendentals=10**3),
        name="last",
    )(*between)


def solution(mesh):
    split = ("gx", "gy")
    return jax.shard_map(
        body,
        mesh=mesh,
        in_specs=(
            P(split, None), P(split, None, None), P(split, None), P(split, None, None), P(split, None, None),
            P(split), P(), P(), P(), P(), P(), P(),
        ),
        out_specs=P(split, None),
        check_vma=False,
    )
```

```python
import functools

import jax
import jax.numpy as jnp
from jax import lax
from jax.experimental import pallas as pl
from jax.experimental.pallas import tpu as pltpu
from jax.sharding import PartitionSpec as P

MESH = pl.DeviceIdType.MESH
F32 = jnp.float32
BF16 = jnp.bfloat16
FAR = 2


def dot(left, right):
    return jnp.dot(left, right, preferred_element_type=F32)


def silu(value):
    return value * jax.nn.sigmoid(value)


def normalised(raw):
    centred = raw - jnp.mean(raw, axis=1, keepdims=True)
    variance = jnp.mean(centred * centred, axis=1, keepdims=True)
    return centred * lax.rsqrt(variance + 1e-05)


def exchange_kernel(
    sources_in, send_x_in, send_y_in, counts, b_node_in, ln_gain_in,
    features, coefficients, w_msg_in, w_msg_out, w_node_in, w_node_out,
    last_hidden, last_states, last_w, last_row,
    sources, send_x, send_y, b_node, ln_gain,
    feat, coef, w_mi, w_mo, w_ni, w_no, merged, states, own, first_states, sent, halo_first, halo_second, base,
    small_sem, load_sem, send_sem, recv_sem,
):
    blocks, size, width = feat.shape
    n_sent = sent.shape[1]
    n_y = send_y.shape[1] * send_y.shape[2]
    near = sources.shape[0] - FAR
    halo = (halo_first, halo_second)
    i, j = lax.axis_index("gx"), lax.axis_index("gy")
    n_i, n_j = lax.axis_size("gx"), lax.axis_size("gy")

    lower_x, upper_x = i > 0, i < n_i - 1
    lower_y, upper_y = j > 0, j < n_j - 1
    routes = [
        ((i, jnp.minimum(j + 1, n_j - 1)), upper_y, lower_y, 0, 2),
        ((i, jnp.maximum(j - 1, 0)), lower_y, upper_y, 2, 4),
        ((jnp.minimum(i + 1, n_i - 1), j), upper_x, lower_x, 4, 5),
        ((jnp.maximum(i - 1, 0), j), lower_x, upper_x, 5, 6),
    ]
    barrier = pltpu.get_barrier_semaphore()
    for device, there, _, _, _ in routes:

        @pl.when(there)
        def _():
            pl.semaphore_signal(barrier, inc=1, device_id=device, device_id_type=MESH)

    smalls = [
        pltpu.make_async_copy(source, target, small_sem.at[n])
        for n, (source, target) in enumerate(
            [
                (sources_in, sources), (send_x_in, send_x), (send_y_in, send_y),
                (b_node_in, b_node), (ln_gain_in, ln_gain),
            ]
        )
    ]
    pairs = {
        "mo0": (w_msg_out.at[0], w_mo.at[0]),
        "far0": (w_node_in.at[0, width:], w_ni.at[0, width:]),
        "feat": (features, feat),
        "mi0": (w_msg_in.at[0], w_mi.at[0]),
        "near0": (w_node_in.at[0, :width], w_ni.at[0, :width]),
        "coef": (coefficients, coef),
        "no0": (w_node_out.at[0], w_no.at[0]),
        "mi1": (w_msg_in.at[1], w_mi.at[1]),
        "mo1": (w_msg_out.at[1], w_mo.at[1]),
        "ni1": (w_node_in.at[1], w_ni.at[1]),
        "no1": (w_node_out.at[1], last_w),
    }
    loads = {
        name: pltpu.make_async_copy(source, target, load_sem.at[n]) for n, (name, (source, target)) in enumerate(pairs.items())
    }
    for name in ("mo0", "far0"):
        loads[name].start()
    for copy in smalls:
        copy.start()
    for name in ("feat", "mi0"):
        loads[name].start()

    for _, _, comes, lo, hi in routes:

        @pl.when(jnp.logical_not(comes))
        def _():
            for buffer in halo:
                buffer[lo:hi] = jnp.zeros((hi - lo, size, width), BF16)

    def transfer(layer, n):
        device, there, comes, lo, hi = routes[n]
        copy = pltpu.make_async_remote_copy(
            src_ref=sent.at[layer, lo:hi],
            dst_ref=halo[layer].at[lo:hi],
            send_sem=send_sem.at[layer, n],
            recv_sem=recv_sem.at[layer, n],
            device_id=device,
            device_id_type=MESH,
        )
        return copy, there, comes

    def start(layer, routes_now):
        for n in routes_now:
            copy, there, _ = transfer(layer, n)
            pl.when(there)(copy.start)

    def receive(layer):
        for n in range(len(routes)):
            copy, _, comes = transfer(layer, n)
            pl.when(comes)(copy.wait_recv)

    def drain(layer):
        for n in range(len(routes)):
            copy, there, _ = transfer(layer, n)
            pl.when(there)(copy.wait_send)

    def merge(layer):
        merged[layer] = dot(w_mo[layer], w_ni[layer, width:]).astype(BF16)

    for name in ("mo0", "far0"):
        loads[name].wait()
    merge(0)
    for copy in smalls:
        copy.wait()
    listed = [send_y[0, side, n] for side in (0, 1) for n in range(2)] + [send_x[0, 0, 0], send_x[0, 0, 1]]
    count = counts[0, 0]
    row = lax.broadcasted_iota(jnp.int32, (size, 1), 0)
    zero = jnp.zeros((), BF16)

    def live(block):
        return row + block * size < count

    def stacked(parts):
        return jnp.concatenate(parts, 0)

    def split(rows):
        return rows.reshape(rows.shape[0] // size, size, width)

    def outgoing(layer, rows):
        return dot(silu(dot(rows, w_mi[layer])).astype(BF16), merged[layer]).astype(BF16)

    def rows_base(layer, rows):
        return split(dot(rows, w_ni[layer, :width]) + b_node[layer][None, :])

    def add_own(layer):
        for block in range(blocks):
            picked = stacked([own[layer, sources[slot, block]] for slot in range(near)])
            base[block] += dot(coef[block, :, : near * size], picked)

    def pool_index(slot, block):
        index = sources[slot, block] - blocks
        return jnp.clip(jnp.where(index < 2, index + n_y, index - 2), 0, n_sent - 1)

    def activated(layer, block):
        picked = stacked([halo[layer][pool_index(slot, block)] for slot in range(near, near + FAR)])
        return silu(base[block] + dot(coef[block, :, near * size :], picked)).astype(BF16)

    def advanced(blocks_now, old):
        raw = dot(stacked([activated(0, block) for block in blocks_now]), w_no[0])
        alive = stacked([live(block) for block in blocks_now])
        return jnp.where(alive, old.astype(F32) + ln_gain[0][None, :] * normalised(raw), 0.0).astype(BF16)

    loads["feat"].wait()
    for n in range(n_sent):
        first_states[n] = jnp.where(live(listed[n]), feat[listed[n]], zero)
    for name in ("near0", "coef", "no0", "mi1", "mo1", "ni1", "no1"):
        loads[name].start()
    loads["mi0"].wait()
    sent[0] = split(outgoing(0, first_states[...].reshape(n_sent * size, width)))
    pl.semaphore_wait(barrier, sum(there.astype(jnp.int32) for _, there, _, _, _ in routes))
    start(0, (0, 1, 2, 3))

    def flat(values):
        return values.reshape(values.shape[0] * size, width)

    halves = [(0, 8), (8, 16)]

    for lo, hi in halves:
        for block in range(lo, hi):
            states[0, block] = jnp.where(live(block), feat[block], zero)
    raws = [dot(flat(states[0, lo:hi]), w_mi[0]) for lo, hi in halves]
    for name in ("near0", "coef"):
        loads[name].wait()
    for (lo, hi), raw in zip(halves, raws):
        base[lo:hi] = rows_base(0, flat(states[0, lo:hi]))
        own[0, lo:hi] = split(dot(silu(raw).astype(BF16), merged[0]).astype(BF16))
    for name in ("no0", "mi1", "mo1", "ni1", "no1"):
        loads[name].wait()
    merge(1)
    add_own(0)

    receive(0)

    def next_states(groups, olds):
        hiddens = [stacked([activated(0, block) for block in group]) for group in groups]
        raws = [dot(value, w_no[0]) for value in hiddens]
        news = []
        for group, old, raw in zip(groups, olds, raws):
            alive = stacked([live(block) for block in group])
            value = old().astype(F32) + ln_gain[0][None, :] * normalised(raw)
            news.append(jnp.where(alive, value, 0.0).astype(BF16))
        return news

    groups = [(0, 1), (2, 3), (4, 5)]
    news = next_states(
        [[listed[n] for n in group] for group in groups],
        [lambda group=group: stacked([first_states[n] for n in group]) for group in groups],
    )
    raws = [dot(new, w_mi[1]) for new in news]
    for group, raw in zip(groups, raws):
        rows = split(dot(silu(raw).astype(BF16), merged[1]).astype(BF16))
        for n, row_block in zip(group, rows):
            sent[1, n] = row_block
    start(1, (0, 1, 2, 3))

    news = next_states(
        [range(lo, hi) for lo, hi in halves], [lambda lo=lo, hi=hi: flat(states[0, lo:hi]) for lo, hi in halves]
    )
    raws = []
    for (lo, hi), new in zip(halves, news):
        last_states[lo * size : hi * size] = new
        raws.append(dot(new, w_mi[1]))
    for (lo, hi), new, raw in zip(halves, news, raws):
        base[lo:hi] = rows_base(1, new)
        own[1, lo:hi] = split(dot(silu(raw).astype(BF16), merged[1]).astype(BF16))
    add_own(1)
    last_row[0:1] = ln_gain[1:2]
    last_row[1:2] = jnp.full((1, width), count, jnp.int32).astype(F32)

    receive(1)
    for block in range(blocks):
        last_hidden[block * size : (block + 1) * size] = activated(1, block)
    drain(0)
    drain(1)


def last_kernel(last_hidden, last_states, last_w, last_row, out, latents, out_sem):
    nodes = last_states.shape[0]
    parts = out_sem.shape[0]
    step = nodes // parts
    gain, count = last_row[0:1], last_row[1:2]
    stores = []
    for n in range(parts):
        rows = slice(n * step, (n + 1) * step)
        normed = normalised(dot(last_hidden[rows], last_w[...]))
        position = lax.broadcasted_iota(jnp.int32, (step, 1), 0) + n * step
        alive = position.astype(F32) < count
        latents[rows] = jnp.where(alive, last_states[rows].astype(F32) + gain * normed, 0.0).astype(BF16)
        store = pltpu.make_async_copy(latents.at[rows], out.at[rows], out_sem.at[n])
        store.start()
        stores.append(store)
    for store in stores:
        store.wait()


def body(
    features, coefficients, source_blocks, send_x, send_y, node_counts,
    w_msg_in, w_msg_out, w_node_in, b_node, w_node_out, ln_gain,
):
    blocks, size, fan = coefficients.shape
    nodes, width = features.shape
    layers = w_msg_in.shape[0]
    n_sent = send_x.shape[1] * send_x.shape[2] + send_y.shape[1] * send_y.shape[2]
    any_, vmem = pl.BlockSpec(memory_space=pl.ANY), pl.BlockSpec(memory_space=pltpu.VMEM)
    operands = [
        source_blocks.T, send_x.transpose(0, 2, 1), send_y, node_counts.reshape(1, 1), b_node, ln_gain,
        features.reshape(blocks, size, width), coefficients, w_msg_in, w_msg_out, w_node_in, w_node_out,
    ]
    operands = [
        operand if operand.size == 1 else pltpu.with_memory_space_constraint(operand, pltpu.HBM) for operand in operands
    ]
    ints = [pltpu.SMEM(operand.shape, jnp.int32) for operand in operands[:3]]
    counted = pl.BlockSpec(memory_space=pltpu.SMEM)
    handed = [((nodes, width), BF16), ((nodes, width), BF16), ((width, width), BF16), ((8, width), F32)]
    between = pl.pallas_call(
        exchange_kernel,
        out_shape=[pltpu.VMEM(shape, dtype) for shape, dtype in handed],
        in_specs=[any_] * 3 + [counted] + [any_] * 8,
        out_specs=[vmem] * len(handed),
        scratch_shapes=ints
        + [
            pltpu.VMEM(b_node.shape, F32),
            pltpu.VMEM(ln_gain.shape, F32),
            pltpu.VMEM((blocks, size, width), BF16),
            pltpu.VMEM((blocks, size, fan), BF16),
            pltpu.VMEM(w_msg_in.shape, BF16),
            pltpu.VMEM(w_msg_out.shape, BF16),
            pltpu.VMEM(w_node_in.shape, BF16),
            pltpu.VMEM((1, width, width), BF16),
            pltpu.VMEM(w_msg_out.shape, BF16),
            pltpu.VMEM((1, blocks, size, width), BF16),
            pltpu.VMEM((layers, blocks, size, width), BF16),
            pltpu.VMEM((n_sent, size, width), BF16),
            pltpu.VMEM((layers, n_sent, size, width), BF16),
            pltpu.VMEM((n_sent, size, width), BF16),
            pltpu.VMEM((n_sent, size, width), BF16),
            pltpu.VMEM((blocks, size, width), F32),
            pltpu.SemaphoreType.DMA((5,)),
            pltpu.SemaphoreType.DMA((11,)),
            pltpu.SemaphoreType.DMA((layers, 4)),
            pltpu.SemaphoreType.DMA((layers, 4)),
        ],
        compiler_params=pltpu.CompilerParams(
            collective_id=0, has_side_effects=True, vmem_limit_bytes=40 * 2**20
        ),
        cost_estimate=pl.CostEstimate(flops=6 * 10**9, bytes_accessed=9 * 2**20, transcendentals=2 * 10**6),
        name="exchange",
    )(*operands)
    return pl.pallas_call(
        last_kernel,
        out_shape=jax.ShapeDtypeStruct((nodes, width), BF16),
        in_specs=[vmem] * len(handed),
        out_specs=any_,
        scratch_shapes=[pltpu.VMEM((nodes, width), BF16), pltpu.SemaphoreType.DMA((4,))],
        compiler_params=pltpu.CompilerParams(vmem_limit_bytes=40 * 2**20),
        cost_estimate=pl.CostEstimate(flops=6 * 10**8, bytes_accessed=2**20, transcendentals=10**3),
        name="last",
    )(*between)


def solution(mesh):
    split = ("gx", "gy")
    return jax.shard_map(
        body,
        mesh=mesh,
        in_specs=(
            P(split, None), P(split, None, None), P(split, None), P(split, None, None), P(split, None, None),
            P(split), P(), P(), P(), P(), P(), P(),
        ),
        out_specs=P(split, None),
        check_vma=False,
    )
```

```python
import functools

import jax
import jax.numpy as jnp
from jax import lax
from jax.experimental import pallas as pl
from jax.experimental.pallas import tpu as pltpu
from jax.sharding import PartitionSpec as P

MESH = pl.DeviceIdType.MESH
F32 = jnp.float32
BF16 = jnp.bfloat16
FAR = 2


def dot(left, right):
    return jnp.dot(left, right, preferred_element_type=F32)


def silu(value):
    return value * jax.nn.sigmoid(value)


def centred(weight):
    weight = weight.astype(F32)
    return (weight - jnp.mean(weight, axis=1, keepdims=True)).astype(BF16)


def normalised(raw):
    return raw * lax.rsqrt(jnp.mean(raw * raw, axis=1, keepdims=True) + 1e-05)


def exchange_kernel(
    sources_in, send_x_in, send_y_in, counts, b_node_in, ln_gain_in,
    features, coefficients, w_msg_in, w_msg_out, w_node_in, w_node_out,
    last_hidden, last_states, last_w, last_row,
    sources, send_x, send_y, b_node, ln_gain,
    feat, coef, w_mi, w_mo, w_ni, w_no, first_w, merged, states, own, first_states, sent, halo_first, halo_second, base,
    small_sem, load_sem, send_sem, recv_sem,
):
    blocks, size, width = feat.shape
    n_sent = sent.shape[1]
    n_y = send_y.shape[1] * send_y.shape[2]
    near = sources.shape[0] - FAR
    halo = (halo_first, halo_second)
    i, j = lax.axis_index("gx"), lax.axis_index("gy")
    n_i, n_j = lax.axis_size("gx"), lax.axis_size("gy")

    lower_x, upper_x = i > 0, i < n_i - 1
    lower_y, upper_y = j > 0, j < n_j - 1
    routes = [
        ((i, jnp.minimum(j + 1, n_j - 1)), upper_y, lower_y, 0, 2),
        ((i, jnp.maximum(j - 1, 0)), lower_y, upper_y, 2, 4),
        ((jnp.minimum(i + 1, n_i - 1), j), upper_x, lower_x, 4, 5),
        ((jnp.maximum(i - 1, 0), j), lower_x, upper_x, 5, 6),
    ]
    barrier = pltpu.get_barrier_semaphore()
    for device, there, _, _, _ in routes:

        @pl.when(there)
        def _():
            pl.semaphore_signal(barrier, inc=1, device_id=device, device_id_type=MESH)

    smalls = [
        pltpu.make_async_copy(source, target, small_sem.at[n])
        for n, (source, target) in enumerate(
            [
                (sources_in, sources), (send_x_in, send_x), (send_y_in, send_y),
                (b_node_in, b_node), (ln_gain_in, ln_gain),
            ]
        )
    ]
    pairs = {
        "mo0": (w_msg_out.at[0], w_mo.at[0]),
        "far0": (w_node_in.at[0, width:], w_ni.at[0, width:]),
        "feat": (features, feat),
        "mi0": (w_msg_in.at[0], w_mi.at[0]),
        "near0": (w_node_in.at[0, :width], w_ni.at[0, :width]),
        "coef": (coefficients, coef),
        "no0": (w_node_out.at[0], w_no.at[0]),
        "mi1": (w_msg_in.at[1], w_mi.at[1]),
        "mo1": (w_msg_out.at[1], w_mo.at[1]),
        "ni1": (w_node_in.at[1], w_ni.at[1]),
        "no1": (w_node_out.at[1], w_no.at[1]),
    }
    loads = {
        name: pltpu.make_async_copy(source, target, load_sem.at[n]) for n, (name, (source, target)) in enumerate(pairs.items())
    }
    for name in ("mo0", "far0"):
        loads[name].start()
    for copy in smalls:
        copy.start()
    for name in ("feat", "mi0"):
        loads[name].start()

    for _, _, comes, lo, hi in routes:

        @pl.when(jnp.logical_not(comes))
        def _():
            for buffer in halo:
                buffer[lo:hi] = jnp.zeros((hi - lo, size, width), BF16)

    def transfer(layer, n):
        device, there, comes, lo, hi = routes[n]
        copy = pltpu.make_async_remote_copy(
            src_ref=sent.at[layer, lo:hi],
            dst_ref=halo[layer].at[lo:hi],
            send_sem=send_sem.at[layer, n],
            recv_sem=recv_sem.at[layer, n],
            device_id=device,
            device_id_type=MESH,
        )
        return copy, there, comes

    def start(layer, routes_now):
        inner = functools.reduce(jnp.logical_and, [route[1] for route in routes])

        @pl.when(inner)
        def _():
            for n in routes_now:
                transfer(layer, n)[0].start()

        @pl.when(jnp.logical_not(inner))
        def _():
            for n in routes_now:
                copy, there, _ = transfer(layer, n)
                pl.when(there)(copy.start)

    def receive(layer):
        inner = functools.reduce(jnp.logical_and, [route[1] for route in routes])

        @pl.when(inner)
        def _():
            for n in range(len(routes)):
                transfer(layer, n)[0].wait_recv()

        @pl.when(jnp.logical_not(inner))
        def _():
            for n in range(len(routes)):
                copy, _, comes = transfer(layer, n)
                pl.when(comes)(copy.wait_recv)

    def drain(layer):
        for n in range(len(routes)):
            copy, there, _ = transfer(layer, n)
            pl.when(there)(copy.wait_send)

    def merge(layer):
        merged[layer] = dot(w_mo[layer], w_ni[layer, width:]).astype(BF16)

    for name in ("mo0", "far0"):
        loads[name].wait()
    merge(0)
    for copy in smalls:
        copy.wait()
    listed = [send_y[0, side, n] for side in (0, 1) for n in range(2)] + [send_x[0, 0, 0], send_x[0, 0, 1]]
    count = counts[0, 0]
    row = lax.broadcasted_iota(jnp.int32, (size, 1), 0)
    zero = jnp.zeros((), BF16)

    def live(block):
        return row + block * size < count

    def stacked(parts):
        return jnp.concatenate(parts, 0)

    def split(rows):
        return rows.reshape(rows.shape[0] // size, size, width)

    def outgoing(layer, rows):
        return dot(silu(dot(rows, w_mi[layer])).astype(BF16), merged[layer]).astype(BF16)

    def rows_base(layer, rows):
        return split(dot(rows, w_ni[layer, :width]) + b_node[layer][None, :])

    def add_own(layer):
        for block in range(blocks):
            picked = stacked([own[layer, sources[slot, block]] for slot in range(near)])
            base[block] += dot(coef[block, :, : near * size], picked)

    def pool_index(slot, block):
        index = sources[slot, block] - blocks
        return jnp.clip(jnp.where(index < 2, index + n_y, index - 2), 0, n_sent - 1)

    def activated(layer, block):
        picked = stacked([halo[layer][pool_index(slot, block)] for slot in range(near, near + FAR)])
        return silu(base[block] + dot(coef[block, :, near * size :], picked)).astype(BF16)

    def advanced(blocks_now, old):
        raw = dot(stacked([activated(0, block) for block in blocks_now]), w_no[0])
        alive = stacked([live(block) for block in blocks_now])
        return jnp.where(alive, old.astype(F32) + ln_gain[0][None, :] * normalised(raw), 0.0).astype(BF16)

    loads["feat"].wait()
    for n in range(n_sent):
        first_states[n] = jnp.where(live(listed[n]), feat[listed[n]], zero)
    for name in ("near0", "coef", "no0", "mi1", "mo1", "ni1", "no1"):
        loads[name].start()
    loads["mi0"].wait()
    sent[0] = split(outgoing(0, first_states[...].reshape(n_sent * size, width)))
    pl.semaphore_wait(barrier, sum(there.astype(jnp.int32) for _, there, _, _, _ in routes))
    start(0, (0, 1, 2, 3))

    def flat(values):
        return values.reshape(values.shape[0] * size, width)

    halves = [(0, 8), (8, 16)]

    for lo, hi in halves:
        for block in range(lo, hi):
            states[0, block] = jnp.where(live(block), feat[block], zero)
    raws = [dot(flat(states[0, lo:hi]), w_mi[0]) for lo, hi in halves]
    for name in ("near0", "coef"):
        loads[name].wait()
    for (lo, hi), raw in zip(halves, raws):
        base[lo:hi] = rows_base(0, flat(states[0, lo:hi]))
        own[0, lo:hi] = split(dot(silu(raw).astype(BF16), merged[0]).astype(BF16))
    for name in ("no0", "mi1", "mo1", "ni1", "no1"):
        loads[name].wait()
    merge(1)
    first_w[...] = centred(w_no[0])
    last_w[...] = centred(w_no[1])
    add_own(0)

    receive(0)

    def next_states(groups, olds):
        hiddens = [stacked([activated(0, block) for block in group]) for group in groups]
        raws = [dot(value, first_w[...]) for value in hiddens]
        news = []
        for group, old, raw in zip(groups, olds, raws):
            alive = stacked([live(block) for block in group])
            value = old().astype(F32) + ln_gain[0][None, :] * normalised(raw)
            news.append(jnp.where(alive, value, 0.0).astype(BF16))
        return news

    groups = [(0, 1), (2, 3), (4, 5)]
    news = next_states(
        [[listed[n] for n in group] for group in groups],
        [lambda group=group: stacked([first_states[n] for n in group]) for group in groups],
    )
    raws = [dot(new, w_mi[1]) for new in news]
    for group, raw in zip(groups, raws):
        rows = split(dot(silu(raw).astype(BF16), merged[1]).astype(BF16))
        for n, row_block in zip(group, rows):
            sent[1, n] = row_block
    start(1, (0, 1, 2, 3))

    news = next_states(
        [range(lo, hi) for lo, hi in halves], [lambda lo=lo, hi=hi: flat(states[0, lo:hi]) for lo, hi in halves]
    )
    raws = []
    for (lo, hi), new in zip(halves, news):
        last_states[lo * size : hi * size] = new
        raws.append(dot(new, w_mi[1]))
    for (lo, hi), new, raw in zip(halves, news, raws):
        base[lo:hi] = rows_base(1, new)
        own[1, lo:hi] = split(dot(silu(raw).astype(BF16), merged[1]).astype(BF16))
    add_own(1)
    last_row[0:1] = ln_gain[1:2]
    last_row[1:2] = jnp.full((1, width), count, jnp.int32).astype(F32)

    receive(1)
    for block in range(blocks):
        last_hidden[block * size : (block + 1) * size] = activated(1, block)
    drain(0)
    drain(1)


def last_kernel(last_hidden, last_states, last_w, last_row, out, latents, out_sem):
    nodes = last_states.shape[0]
    parts = out_sem.shape[0]
    step = nodes // parts
    gain, count = last_row[0:1], last_row[1:2]
    stores = []
    for n in range(parts):
        rows = slice(n * step, (n + 1) * step)
        normed = normalised(dot(last_hidden[rows], last_w[...]))
        position = lax.broadcasted_iota(jnp.int32, (step, 1), 0) + n * step
        alive = position.astype(F32) < count
        latents[rows] = jnp.where(alive, last_states[rows].astype(F32) + gain * normed, 0.0).astype(BF16)
        store = pltpu.make_async_copy(latents.at[rows], out.at[rows], out_sem.at[n])
        store.start()
        stores.append(store)
    for store in stores:
        store.wait()


def body(
    features, coefficients, source_blocks, send_x, send_y, node_counts,
    w_msg_in, w_msg_out, w_node_in, b_node, w_node_out, ln_gain,
):
    blocks, size, fan = coefficients.shape
    nodes, width = features.shape
    layers = w_msg_in.shape[0]
    n_sent = send_x.shape[1] * send_x.shape[2] + send_y.shape[1] * send_y.shape[2]
    any_, vmem = pl.BlockSpec(memory_space=pl.ANY), pl.BlockSpec(memory_space=pltpu.VMEM)
    operands = [
        source_blocks.T, send_x.transpose(0, 2, 1), send_y, node_counts.reshape(1, 1), b_node, ln_gain,
        features.reshape(blocks, size, width), coefficients, w_msg_in, w_msg_out, w_node_in, w_node_out,
    ]
    operands = [
        operand if operand.size == 1 else pltpu.with_memory_space_constraint(operand, pltpu.HBM) for operand in operands
    ]
    ints = [pltpu.SMEM(operand.shape, jnp.int32) for operand in operands[:3]]
    counted = pl.BlockSpec(memory_space=pltpu.SMEM)
    handed = [((nodes, width), BF16), ((nodes, width), BF16), ((width, width), BF16), ((8, width), F32)]
    between = pl.pallas_call(
        exchange_kernel,
        out_shape=[pltpu.VMEM(shape, dtype) for shape, dtype in handed],
        in_specs=[any_] * 3 + [counted] + [any_] * 8,
        out_specs=[vmem] * len(handed),
        scratch_shapes=ints
        + [
            pltpu.VMEM(b_node.shape, F32),
            pltpu.VMEM(ln_gain.shape, F32),
            pltpu.VMEM((blocks, size, width), BF16),
            pltpu.VMEM((blocks, size, fan), BF16),
            pltpu.VMEM(w_msg_in.shape, BF16),
            pltpu.VMEM(w_msg_out.shape, BF16),
            pltpu.VMEM(w_node_in.shape, BF16),
            pltpu.VMEM(w_node_out.shape, BF16),
            pltpu.VMEM((width, width), BF16),
            pltpu.VMEM(w_msg_out.shape, BF16),
            pltpu.VMEM((1, blocks, size, width), BF16),
            pltpu.VMEM((layers, blocks, size, width), BF16),
            pltpu.VMEM((n_sent, size, width), BF16),
            pltpu.VMEM((layers, n_sent, size, width), BF16),
            pltpu.VMEM((n_sent, size, width), BF16),
            pltpu.VMEM((n_sent, size, width), BF16),
            pltpu.VMEM((blocks, size, width), F32),
            pltpu.SemaphoreType.DMA((5,)),
            pltpu.SemaphoreType.DMA((11,)),
            pltpu.SemaphoreType.DMA((layers, 4)),
            pltpu.SemaphoreType.DMA((layers, 4)),
        ],
        compiler_params=pltpu.CompilerParams(
            collective_id=0, has_side_effects=True, vmem_limit_bytes=40 * 2**20
        ),
        cost_estimate=pl.CostEstimate(flops=6 * 10**9, bytes_accessed=9 * 2**20, transcendentals=2 * 10**6),
        name="exchange",
    )(*operands)
    return pl.pallas_call(
        last_kernel,
        out_shape=jax.ShapeDtypeStruct((nodes, width), BF16),
        in_specs=[vmem] * len(handed),
        out_specs=any_,
        scratch_shapes=[pltpu.VMEM((nodes, width), BF16), pltpu.SemaphoreType.DMA((4,))],
        compiler_params=pltpu.CompilerParams(vmem_limit_bytes=40 * 2**20),
        cost_estimate=pl.CostEstimate(flops=6 * 10**8, bytes_accessed=2**20, transcendentals=10**3),
        name="last",
    )(*between)


def solution(mesh):
    split = ("gx", "gy")
    return jax.shard_map(
        body,
        mesh=mesh,
        in_specs=(
            P(split, None), P(split, None, None), P(split, None), P(split, None, None), P(split, None, None),
            P(split), P(), P(), P(), P(), P(), P(),
        ),
        out_specs=P(split, None),
        check_vma=False,
    )
```

```python
import functools

import jax
import jax.numpy as jnp
from jax import lax
from jax.experimental import pallas as pl
from jax.experimental.pallas import tpu as pltpu
from jax.sharding import PartitionSpec as P

MESH = pl.DeviceIdType.MESH
F32 = jnp.float32
BF16 = jnp.bfloat16
FAR = 2


def dot(left, right):
    return jnp.dot(left, right, preferred_element_type=F32)


def silu(value):
    return value * jax.nn.sigmoid(value)


def centred(weight):
    weight = weight.astype(F32)
    return (weight - jnp.mean(weight, axis=1, keepdims=True)).astype(BF16)


def normalised(raw):
    return raw * lax.rsqrt(jnp.mean(raw * raw, axis=1, keepdims=True) + 1e-05)


def exchange_kernel(
    sources_in, send_x_in, send_y_in, counts, b_node_in, ln_gain_in,
    features, coefficients, w_msg_in, w_msg_out, w_node_in, w_node_out,
    halo_second, base, coef, last_states, last_w, last_row, picks,
    sources, send_x, send_y, b_node, ln_gain,
    feat, w_mi, w_mo, w_ni, w_no, first_w, merged, states, own, first_states, sent, halo_first,
    small_sem, load_sem, send_sem, recv_sem,
):
    blocks, size, width = feat.shape
    n_sent = sent.shape[1]
    n_y = send_y.shape[1] * send_y.shape[2]
    near = sources.shape[0] - FAR
    halo = (halo_first, halo_second)
    i, j = lax.axis_index("gx"), lax.axis_index("gy")
    n_i, n_j = lax.axis_size("gx"), lax.axis_size("gy")

    lower_x, upper_x = i > 0, i < n_i - 1
    lower_y, upper_y = j > 0, j < n_j - 1
    routes = [
        ((i, jnp.minimum(j + 1, n_j - 1)), upper_y, lower_y, 0, 2),
        ((i, jnp.maximum(j - 1, 0)), lower_y, upper_y, 2, 4),
        ((jnp.minimum(i + 1, n_i - 1), j), upper_x, lower_x, 4, 5),
        ((jnp.maximum(i - 1, 0), j), lower_x, upper_x, 5, 6),
    ]
    barrier = pltpu.get_barrier_semaphore()
    for device, there, _, _, _ in routes:

        @pl.when(there)
        def _():
            pl.semaphore_signal(barrier, inc=1, device_id=device, device_id_type=MESH)

    smalls = [
        pltpu.make_async_copy(source, target, small_sem.at[n])
        for n, (source, target) in enumerate(
            [
                (sources_in, sources), (send_x_in, send_x), (send_y_in, send_y),
                (b_node_in, b_node), (ln_gain_in, ln_gain),
            ]
        )
    ]
    pairs = {
        "mo0": (w_msg_out.at[0], w_mo.at[0]),
        "far0": (w_node_in.at[0, width:], w_ni.at[0, width:]),
        "feat": (features, feat),
        "mi0": (w_msg_in.at[0], w_mi.at[0]),
        "near0": (w_node_in.at[0, :width], w_ni.at[0, :width]),
        "coef": (coefficients, coef),
        "no0": (w_node_out.at[0], w_no.at[0]),
        "mi1": (w_msg_in.at[1], w_mi.at[1]),
        "mo1": (w_msg_out.at[1], w_mo.at[1]),
        "ni1": (w_node_in.at[1], w_ni.at[1]),
        "no1": (w_node_out.at[1], w_no.at[1]),
    }
    loads = {
        name: pltpu.make_async_copy(source, target, load_sem.at[n]) for n, (name, (source, target)) in enumerate(pairs.items())
    }
    for name in ("mo0", "far0"):
        loads[name].start()
    for copy in smalls:
        copy.start()
    for name in ("feat", "mi0"):
        loads[name].start()

    for _, _, comes, lo, hi in routes:

        @pl.when(jnp.logical_not(comes))
        def _():
            for buffer in halo:
                buffer[lo:hi] = jnp.zeros((hi - lo, size, width), BF16)

    def transfer(layer, n):
        device, there, comes, lo, hi = routes[n]
        copy = pltpu.make_async_remote_copy(
            src_ref=sent.at[layer, lo:hi],
            dst_ref=halo[layer].at[lo:hi],
            send_sem=send_sem.at[layer, n],
            recv_sem=recv_sem.at[layer, n],
            device_id=device,
            device_id_type=MESH,
        )
        return copy, there, comes

    def start(layer, routes_now):
        inner = functools.reduce(jnp.logical_and, [route[1] for route in routes])

        @pl.when(inner)
        def _():
            for n in routes_now:
                transfer(layer, n)[0].start()

        @pl.when(jnp.logical_not(inner))
        def _():
            for n in routes_now:
                copy, there, _ = transfer(layer, n)
                pl.when(there)(copy.start)

    def receive(layer):
        inner = functools.reduce(jnp.logical_and, [route[1] for route in routes])

        @pl.when(inner)
        def _():
            for n in range(len(routes)):
                transfer(layer, n)[0].wait_recv()

        @pl.when(jnp.logical_not(inner))
        def _():
            for n in range(len(routes)):
                copy, _, comes = transfer(layer, n)
                pl.when(comes)(copy.wait_recv)

    def drain(layer):
        for n in range(len(routes)):
            copy, there, _ = transfer(layer, n)
            pl.when(there)(copy.wait_send)

    def merge(layer):
        merged[layer] = dot(w_mo[layer], w_ni[layer, width:]).astype(BF16)

    for name in ("mo0", "far0"):
        loads[name].wait()
    merge(0)
    for copy in smalls:
        copy.wait()
    listed = [send_y[0, side, n] for side in (0, 1) for n in range(2)] + [send_x[0, 0, 0], send_x[0, 0, 1]]
    count = counts[0, 0]
    row = lax.broadcasted_iota(jnp.int32, (size, 1), 0)
    zero = jnp.zeros((), BF16)

    def live(block):
        return row + block * size < count

    def stacked(parts):
        return jnp.concatenate(parts, 0)

    def split(rows):
        return rows.reshape(rows.shape[0] // size, size, width)

    def outgoing(layer, rows):
        return dot(silu(dot(rows, w_mi[layer])).astype(BF16), merged[layer]).astype(BF16)

    def rows_base(layer, rows):
        return split(dot(rows, w_ni[layer, :width]) + b_node[layer][None, :])

    def add_own(layer):
        for block in range(blocks):
            picked = stacked([own[layer, sources[slot, block]] for slot in range(near)])
            base[block] += dot(coef[block, :, : near * size], picked)

    def pool_index(slot, block):
        index = sources[slot, block] - blocks
        return jnp.clip(jnp.where(index < 2, index + n_y, index - 2), 0, n_sent - 1)

    def activated(layer, block):
        picked = stacked([halo[layer][pool_index(slot, block)] for slot in range(near, near + FAR)])
        return silu(base[block] + dot(coef[block, :, near * size :], picked)).astype(BF16)

    def advanced(blocks_now, old):
        raw = dot(stacked([activated(0, block) for block in blocks_now]), w_no[0])
        alive = stacked([live(block) for block in blocks_now])
        return jnp.where(alive, old.astype(F32) + ln_gain[0][None, :] * normalised(raw), 0.0).astype(BF16)

    loads["feat"].wait()
    for n in range(n_sent):
        first_states[n] = jnp.where(live(listed[n]), feat[listed[n]], zero)
    for name in ("near0", "coef", "no0", "mi1", "mo1", "ni1", "no1"):
        loads[name].start()
    loads["mi0"].wait()
    sent[0] = split(outgoing(0, first_states[...].reshape(n_sent * size, width)))
    pl.semaphore_wait(barrier, sum(there.astype(jnp.int32) for _, there, _, _, _ in routes))
    start(0, (0, 1, 2, 3))

    def flat(values):
        return values.reshape(values.shape[0] * size, width)

    halves = [(0, 8), (8, 16)]

    for lo, hi in halves:
        for block in range(lo, hi):
            states[0, block] = jnp.where(live(block), feat[block], zero)
    raws = [dot(flat(states[0, lo:hi]), w_mi[0]) for lo, hi in halves]
    for name in ("near0", "coef"):
        loads[name].wait()
    for (lo, hi), raw in zip(halves, raws):
        base[lo:hi] = rows_base(0, flat(states[0, lo:hi]))
        own[0, lo:hi] = split(dot(silu(raw).astype(BF16), merged[0]).astype(BF16))
    for name in ("no0", "mi1", "mo1", "ni1", "no1"):
        loads[name].wait()
    merge(1)
    first_w[...] = centred(w_no[0])
    last_w[...] = centred(w_no[1])
    add_own(0)

    receive(0)

    def next_states(groups, olds):
        hiddens = [stacked([activated(0, block) for block in group]) for group in groups]
        raws = [dot(value, first_w[...]) for value in hiddens]
        news = []
        for group, old, raw in zip(groups, olds, raws):
            alive = stacked([live(block) for block in group])
            value = old().astype(F32) + ln_gain[0][None, :] * normalised(raw)
            news.append(jnp.where(alive, value, 0.0).astype(BF16))
        return news

    groups = [(0, 1), (2, 3), (4, 5)]
    news = next_states(
        [[listed[n] for n in group] for group in groups],
        [lambda group=group: stacked([first_states[n] for n in group]) for group in groups],
    )
    raws = [dot(new, w_mi[1]) for new in news]
    for group, raw in zip(groups, raws):
        rows = split(dot(silu(raw).astype(BF16), merged[1]).astype(BF16))
        for n, row_block in zip(group, rows):
            sent[1, n] = row_block
    start(1, (0, 1, 2, 3))

    news = next_states(
        [range(lo, hi) for lo, hi in halves], [lambda lo=lo, hi=hi: flat(states[0, lo:hi]) for lo, hi in halves]
    )
    raws = []
    for (lo, hi), new in zip(halves, news):
        last_states[lo * size : hi * size] = new
        raws.append(dot(new, w_mi[1]))
    for (lo, hi), new, raw in zip(halves, news, raws):
        base[lo:hi] = rows_base(1, new)
        own[1, lo:hi] = split(dot(silu(raw).astype(BF16), merged[1]).astype(BF16))
    add_own(1)
    last_row[0:1] = ln_gain[1:2]
    last_row[1:2] = jnp.full((1, width), count, jnp.int32).astype(F32)

    for block in range(blocks):
        for slot in range(near, near + FAR):
            picks[slot - near, block] = pool_index(slot, block)
    receive(1)
    drain(0)
    drain(1)


def last_kernel(halo, base, coef, last_states, last_w, last_row, picks, out, latents, out_sem):
    blocks, size, width = base.shape
    near = coef.shape[2] - FAR * size
    gain, count = last_row[0:1], last_row[1:2]
    parts = out_sem.shape[0]
    step = blocks // parts

    def activated(block):
        picked = jnp.concatenate([halo[picks[slot, block]] for slot in range(FAR)], 0)
        return silu(base[block] + dot(coef[block, :, near:], picked)).astype(BF16)

    hiddens = [jnp.concatenate([activated(block) for block in range(n * step, (n + 1) * step)], 0) for n in range(parts)]
    raws = [dot(value, last_w[...]) for value in hiddens]
    stores = []
    for n, raw in enumerate(raws):
        rows = slice(n * step * size, (n + 1) * step * size)
        position = lax.broadcasted_iota(jnp.int32, (step * size, 1), 0) + n * step * size
        alive = position.astype(F32) < count
        value = last_states[rows].astype(F32) + gain * normalised(raw)
        latents[rows] = jnp.where(alive, value, 0.0).astype(BF16)
        store = pltpu.make_async_copy(latents.at[rows], out.at[rows], out_sem.at[n])
        store.start()
        stores.append(store)
    for store in stores:
        store.wait()


def body(
    features, coefficients, source_blocks, send_x, send_y, node_counts,
    w_msg_in, w_msg_out, w_node_in, b_node, w_node_out, ln_gain,
):
    blocks, size, _ = coefficients.shape
    nodes, width = features.shape
    layers = w_msg_in.shape[0]
    n_sent = send_x.shape[1] * send_x.shape[2] + send_y.shape[1] * send_y.shape[2]
    any_, vmem = pl.BlockSpec(memory_space=pl.ANY), pl.BlockSpec(memory_space=pltpu.VMEM)
    operands = [
        source_blocks.T, send_x.transpose(0, 2, 1), send_y, node_counts.reshape(1, 1), b_node, ln_gain,
        features.reshape(blocks, size, width), coefficients, w_msg_in, w_msg_out, w_node_in, w_node_out,
    ]
    operands = [
        operand if operand.size == 1 else pltpu.with_memory_space_constraint(operand, pltpu.HBM) for operand in operands
    ]
    ints = [pltpu.SMEM(operand.shape, jnp.int32) for operand in operands[:3]]
    counted = pl.BlockSpec(memory_space=pltpu.SMEM)
    handed = [
        pltpu.VMEM((n_sent, size, width), BF16),
        pltpu.VMEM((blocks, size, width), F32),
        pltpu.VMEM(coefficients.shape, BF16),
        pltpu.VMEM((nodes, width), BF16),
        pltpu.VMEM((width, width), BF16),
        pltpu.VMEM((8, width), F32),
        pltpu.SMEM((FAR, blocks), jnp.int32),
    ]
    spaces = [vmem] * 6 + [pl.BlockSpec(memory_space=pltpu.SMEM)]
    between = pl.pallas_call(
        exchange_kernel,
        out_shape=handed,
        in_specs=[any_] * 3 + [counted] + [any_] * 8,
        out_specs=spaces,
        scratch_shapes=ints
        + [
            pltpu.VMEM(b_node.shape, F32),
            pltpu.VMEM(ln_gain.shape, F32),
            pltpu.VMEM((blocks, size, width), BF16),
            pltpu.VMEM(w_msg_in.shape, BF16),
            pltpu.VMEM(w_msg_out.shape, BF16),
            pltpu.VMEM(w_node_in.shape, BF16),
            pltpu.VMEM(w_node_out.shape, BF16),
            pltpu.VMEM((width, width), BF16),
            pltpu.VMEM(w_msg_out.shape, BF16),
            pltpu.VMEM((1, blocks, size, width), BF16),
            pltpu.VMEM((layers, blocks, size, width), BF16),
            pltpu.VMEM((n_sent, size, width), BF16),
            pltpu.VMEM((layers, n_sent, size, width), BF16),
            pltpu.VMEM((n_sent, size, width), BF16),
            pltpu.SemaphoreType.DMA((5,)),
            pltpu.SemaphoreType.DMA((11,)),
            pltpu.SemaphoreType.DMA((layers, 4)),
            pltpu.SemaphoreType.DMA((layers, 4)),
        ],
        compiler_params=pltpu.CompilerParams(
            collective_id=0, has_side_effects=True, vmem_limit_bytes=40 * 2**20
        ),
        cost_estimate=pl.CostEstimate(flops=6 * 10**9, bytes_accessed=9 * 2**20, transcendentals=2 * 10**6),
        name="exchange",
    )(*operands)
    return pl.pallas_call(
        last_kernel,
        out_shape=jax.ShapeDtypeStruct((nodes, width), BF16),
        in_specs=spaces,
        out_specs=any_,
        scratch_shapes=[pltpu.VMEM((nodes, width), BF16), pltpu.SemaphoreType.DMA((4,))],
        compiler_params=pltpu.CompilerParams(vmem_limit_bytes=40 * 2**20),
        cost_estimate=pl.CostEstimate(flops=6 * 10**8, bytes_accessed=2**20, transcendentals=10**3),
        name="last",
    )(*between)


def solution(mesh):
    split = ("gx", "gy")
    return jax.shard_map(
        body,
        mesh=mesh,
        in_specs=(
            P(split, None), P(split, None, None), P(split, None), P(split, None, None), P(split, None, None),
            P(split), P(), P(), P(), P(), P(), P(),
        ),
        out_specs=P(split, None),
        check_vma=False,
    )
```

```python
import functools

import jax
import jax.numpy as jnp
from jax import lax
from jax.experimental import pallas as pl
from jax.experimental.pallas import tpu as pltpu
from jax.sharding import PartitionSpec as P

MESH = pl.DeviceIdType.MESH
F32 = jnp.float32
BF16 = jnp.bfloat16
FAR = 2


def dot(left, right):
    return jnp.dot(left, right, preferred_element_type=F32)


def silu(value):
    return value * jax.nn.sigmoid(value)


def centred(weight):
    weight = weight.astype(F32)
    return (weight - jnp.mean(weight, axis=1, keepdims=True)).astype(BF16)


def normalised(raw):
    return raw * lax.rsqrt(jnp.mean(raw * raw, axis=1, keepdims=True) + 1e-05)


def exchange_kernel(
    sources_in, send_x_in, send_y_in, counts, b_node_in, ln_gain_in,
    features, coefficients, w_msg_in, w_msg_out, w_node_in, w_node_out,
    halo_second, base, coef, last_states, last_w, last_row, picks,
    sources, send_x, send_y, b_node, ln_gain,
    feat, w_mi, w_mo, w_ni, w_no, first_w, merged, states, own, first_states, sent, halo_first,
    small_sem, load_sem, send_sem, recv_sem,
):
    blocks, size, width = feat.shape
    n_sent = sent.shape[1]
    n_y = send_y.shape[1] * send_y.shape[2]
    near = sources.shape[0] - FAR
    halo = (halo_first, halo_second)
    i, j = lax.axis_index("gx"), lax.axis_index("gy")
    n_i, n_j = lax.axis_size("gx"), lax.axis_size("gy")

    lower_x, upper_x = i > 0, i < n_i - 1
    lower_y, upper_y = j > 0, j < n_j - 1
    routes = [
        ((i, jnp.minimum(j + 1, n_j - 1)), upper_y, lower_y, 0, 2),
        ((i, jnp.maximum(j - 1, 0)), lower_y, upper_y, 2, 4),
        ((jnp.minimum(i + 1, n_i - 1), j), upper_x, lower_x, 4, 5),
        ((jnp.maximum(i - 1, 0), j), lower_x, upper_x, 5, 6),
    ]
    barrier = pltpu.get_barrier_semaphore()
    for device, there, _, _, _ in routes:

        @pl.when(there)
        def _():
            pl.semaphore_signal(barrier, inc=1, device_id=device, device_id_type=MESH)

    smalls = [
        pltpu.make_async_copy(source, target, small_sem.at[n])
        for n, (source, target) in enumerate(
            [
                (sources_in, sources), (send_x_in, send_x), (send_y_in, send_y),
                (b_node_in, b_node), (ln_gain_in, ln_gain),
            ]
        )
    ]
    pairs = {
        "mo0": (w_msg_out.at[0], w_mo.at[0]),
        "far0": (w_node_in.at[0, width:], w_ni.at[0, width:]),
        "feat": (features, feat),
        "mi0": (w_msg_in.at[0], w_mi.at[0]),
        "near0": (w_node_in.at[0, :width], w_ni.at[0, :width]),
        "coef": (coefficients, coef),
        "no0": (w_node_out.at[0], w_no.at[0]),
        "mi1": (w_msg_in.at[1], w_mi.at[1]),
        "mo1": (w_msg_out.at[1], w_mo.at[1]),
        "ni1": (w_node_in.at[1], w_ni.at[1]),
        "no1": (w_node_out.at[1], w_no.at[1]),
    }
    loads = {
        name: pltpu.make_async_copy(source, target, load_sem.at[n]) for n, (name, (source, target)) in enumerate(pairs.items())
    }
    for name in ("mo0", "far0"):
        loads[name].start()
    for copy in smalls:
        copy.start()
    for name in ("feat", "mi0"):
        loads[name].start()

    for _, _, comes, lo, hi in routes:

        @pl.when(jnp.logical_not(comes))
        def _():
            for buffer in halo:
                buffer[lo:hi] = jnp.zeros((hi - lo, size, width), BF16)

    def transfer(layer, n):
        device, there, comes, lo, hi = routes[n]
        copy = pltpu.make_async_remote_copy(
            src_ref=sent.at[layer, lo:hi],
            dst_ref=halo[layer].at[lo:hi],
            send_sem=send_sem.at[layer, n],
            recv_sem=recv_sem.at[layer, n],
            device_id=device,
            device_id_type=MESH,
        )
        return copy, there, comes

    def start(layer, routes_now):
        inner = functools.reduce(jnp.logical_and, [route[1] for route in routes])

        @pl.when(inner)
        def _():
            for n in routes_now:
                transfer(layer, n)[0].start()

        @pl.when(jnp.logical_not(inner))
        def _():
            for n in routes_now:
                copy, there, _ = transfer(layer, n)
                pl.when(there)(copy.start)

    def receive(layer):
        inner = functools.reduce(jnp.logical_and, [route[1] for route in routes])

        @pl.when(inner)
        def _():
            for n in range(len(routes)):
                transfer(layer, n)[0].wait_recv()

        @pl.when(jnp.logical_not(inner))
        def _():
            for n in range(len(routes)):
                copy, _, comes = transfer(layer, n)
                pl.when(comes)(copy.wait_recv)

    def drain(layer):
        for n in range(len(routes)):
            copy, there, _ = transfer(layer, n)
            pl.when(there)(copy.wait_send)

    def merge(layer):
        merged[layer] = dot(w_mo[layer], w_ni[layer, width:]).astype(BF16)

    for name in ("mo0", "far0"):
        loads[name].wait()
    merge(0)
    for copy in smalls:
        copy.wait()
    listed = [send_y[0, side, n] for side in (0, 1) for n in range(2)] + [send_x[0, 0, 0], send_x[0, 0, 1]]
    count = counts[0, 0]
    row = lax.broadcasted_iota(jnp.int32, (size, 1), 0)
    zero = jnp.zeros((), BF16)

    def live(block):
        return row + block * size < count

    def stacked(parts):
        return jnp.concatenate(parts, 0)

    def split(rows):
        return rows.reshape(rows.shape[0] // size, size, width)

    def outgoing(layer, rows):
        return dot(silu(dot(rows, w_mi[layer])).astype(BF16), merged[layer]).astype(BF16)

    def rows_base(layer, rows):
        return split(dot(rows, w_ni[layer, :width]) + b_node[layer][None, :])

    def add_own(layer):
        for block in range(blocks):
            picked = stacked([own[layer, sources[slot, block]] for slot in range(near)])
            base[block] += dot(coef[block, :, : near * size], picked)

    def pool_index(slot, block):
        index = sources[slot, block] - blocks
        return jnp.clip(jnp.where(index < 2, index + n_y, index - 2), 0, n_sent - 1)

    def activated(layer, block):
        picked = stacked([halo[layer][pool_index(slot, block)] for slot in range(near, near + FAR)])
        return silu(base[block] + dot(coef[block, :, near * size :], picked)).astype(BF16)

    def advanced(blocks_now, old):
        raw = dot(stacked([activated(0, block) for block in blocks_now]), w_no[0])
        alive = stacked([live(block) for block in blocks_now])
        return jnp.where(alive, old.astype(F32) + ln_gain[0][None, :] * normalised(raw), 0.0).astype(BF16)

    loads["feat"].wait()
    for n in range(n_sent):
        first_states[n] = jnp.where(live(listed[n]), feat[listed[n]], zero)
    for name in ("near0", "coef", "no0", "mi1", "mo1", "ni1", "no1"):
        loads[name].start()
    loads["mi0"].wait()
    sent[0] = split(outgoing(0, first_states[...].reshape(n_sent * size, width)))
    pl.semaphore_wait(barrier, sum(there.astype(jnp.int32) for _, there, _, _, _ in routes))
    start(0, (0, 1, 2, 3))

    def flat(values):
        return values.reshape(values.shape[0] * size, width)

    halves = [(0, 16)]

    for lo, hi in halves:
        for block in range(lo, hi):
            states[0, block] = jnp.where(live(block), feat[block], zero)
    raws = [dot(flat(states[0, lo:hi]), w_mi[0]) for lo, hi in halves]
    for name in ("near0", "coef"):
        loads[name].wait()
    for (lo, hi), raw in zip(halves, raws):
        base[lo:hi] = rows_base(0, flat(states[0, lo:hi]))
        own[0, lo:hi] = split(dot(silu(raw).astype(BF16), merged[0]).astype(BF16))
    for name in ("no0", "mi1", "mo1", "ni1", "no1"):
        loads[name].wait()
    merge(1)
    first_w[...] = centred(w_no[0])
    last_w[...] = centred(w_no[1])
    add_own(0)

    receive(0)

    def next_states(groups, olds):
        hiddens = [stacked([activated(0, block) for block in group]) for group in groups]
        raws = [dot(value, first_w[...]) for value in hiddens]
        news = []
        for group, old, raw in zip(groups, olds, raws):
            alive = stacked([live(block) for block in group])
            value = old().astype(F32) + ln_gain[0][None, :] * normalised(raw)
            news.append(jnp.where(alive, value, 0.0).astype(BF16))
        return news

    groups = [(0, 1), (2, 3), (4, 5)]
    news = next_states(
        [[listed[n] for n in group] for group in groups],
        [lambda group=group: stacked([first_states[n] for n in group]) for group in groups],
    )
    raws = [dot(new, w_mi[1]) for new in news]
    for group, raw in zip(groups, raws):
        rows = split(dot(silu(raw).astype(BF16), merged[1]).astype(BF16))
        for n, row_block in zip(group, rows):
            sent[1, n] = row_block
    start(1, (0, 1, 2, 3))

    news = next_states(
        [range(lo, hi) for lo, hi in halves], [lambda lo=lo, hi=hi: flat(states[0, lo:hi]) for lo, hi in halves]
    )
    raws = []
    for (lo, hi), new in zip(halves, news):
        last_states[lo * size : hi * size] = new
        raws.append(dot(new, w_mi[1]))
    for (lo, hi), new, raw in zip(halves, news, raws):
        base[lo:hi] = rows_base(1, new)
        own[1, lo:hi] = split(dot(silu(raw).astype(BF16), merged[1]).astype(BF16))
    add_own(1)
    drain(0)
    last_row[0:1] = ln_gain[1:2]
    last_row[1:2] = jnp.full((1, width), count, jnp.int32).astype(F32)

    for block in range(blocks):
        for slot in range(near, near + FAR):
            picks[slot - near, block] = pool_index(slot, block)
    receive(1)
    drain(1)


def last_kernel(halo, base, coef, last_states, last_w, last_row, picks, out, latents, out_sem):
    blocks, size, width = base.shape
    near = coef.shape[2] - FAR * size
    gain, count = last_row[0:1], last_row[1:2]
    parts = out_sem.shape[0]
    step = blocks // parts

    def activated(block):
        picked = jnp.concatenate([halo[picks[slot, block]] for slot in range(FAR)], 0)
        return silu(base[block] + dot(coef[block, :, near:], picked)).astype(BF16)

    hiddens = [jnp.concatenate([activated(block) for block in range(n * step, (n + 1) * step)], 0) for n in range(parts)]
    raws = [dot(value, last_w[...]) for value in hiddens]
    stores = []
    for n, raw in enumerate(raws):
        rows = slice(n * step * size, (n + 1) * step * size)
        position = lax.broadcasted_iota(jnp.int32, (step * size, 1), 0) + n * step * size
        alive = position.astype(F32) < count
        value = last_states[rows].astype(F32) + gain * normalised(raw)
        latents[rows] = jnp.where(alive, value, 0.0).astype(BF16)
        store = pltpu.make_async_copy(latents.at[rows], out.at[rows], out_sem.at[n])
        store.start()
        stores.append(store)
    for store in stores:
        store.wait()


def body(
    features, coefficients, source_blocks, send_x, send_y, node_counts,
    w_msg_in, w_msg_out, w_node_in, b_node, w_node_out, ln_gain,
):
    blocks, size, _ = coefficients.shape
    nodes, width = features.shape
    layers = w_msg_in.shape[0]
    n_sent = send_x.shape[1] * send_x.shape[2] + send_y.shape[1] * send_y.shape[2]
    any_, vmem = pl.BlockSpec(memory_space=pl.ANY), pl.BlockSpec(memory_space=pltpu.VMEM)
    operands = [
        source_blocks.T, send_x.transpose(0, 2, 1), send_y, node_counts.reshape(1, 1), b_node, ln_gain,
        features.reshape(blocks, size, width), coefficients, w_msg_in, w_msg_out, w_node_in, w_node_out,
    ]
    operands = [
        operand if operand.size == 1 else pltpu.with_memory_space_constraint(operand, pltpu.HBM) for operand in operands
    ]
    ints = [pltpu.SMEM(operand.shape, jnp.int32) for operand in operands[:3]]
    counted = pl.BlockSpec(memory_space=pltpu.SMEM)
    handed = [
        pltpu.VMEM((n_sent, size, width), BF16),
        pltpu.VMEM((blocks, size, width), F32),
        pltpu.VMEM(coefficients.shape, BF16),
        pltpu.VMEM((nodes, width), BF16),
        pltpu.VMEM((width, width), BF16),
        pltpu.VMEM((8, width), F32),
        pltpu.SMEM((FAR, blocks), jnp.int32),
    ]
    spaces = [vmem] * 6 + [pl.BlockSpec(memory_space=pltpu.SMEM)]
    between = pl.pallas_call(
        exchange_kernel,
        out_shape=handed,
        in_specs=[any_] * 3 + [counted] + [any_] * 8,
        out_specs=spaces,
        scratch_shapes=ints
        + [
            pltpu.VMEM(b_node.shape, F32),
            pltpu.VMEM(ln_gain.shape, F32),
            pltpu.VMEM((blocks, size, width), BF16),
            pltpu.VMEM(w_msg_in.shape, BF16),
            pltpu.VMEM(w_msg_out.shape, BF16),
            pltpu.VMEM(w_node_in.shape, BF16),
            pltpu.VMEM(w_node_out.shape, BF16),
            pltpu.VMEM((width, width), BF16),
            pltpu.VMEM(w_msg_out.shape, BF16),
            pltpu.VMEM((1, blocks, size, width), BF16),
            pltpu.VMEM((layers, blocks, size, width), BF16),
            pltpu.VMEM((n_sent, size, width), BF16),
            pltpu.VMEM((layers, n_sent, size, width), BF16),
            pltpu.VMEM((n_sent, size, width), BF16),
            pltpu.SemaphoreType.DMA((5,)),
            pltpu.SemaphoreType.DMA((11,)),
            pltpu.SemaphoreType.DMA((layers, 4)),
            pltpu.SemaphoreType.DMA((layers, 4)),
        ],
        compiler_params=pltpu.CompilerParams(
            collective_id=0, has_side_effects=True, vmem_limit_bytes=40 * 2**20
        ),
        cost_estimate=pl.CostEstimate(flops=6 * 10**9, bytes_accessed=9 * 2**20, transcendentals=2 * 10**6),
        name="exchange",
    )(*operands)
    return pl.pallas_call(
        last_kernel,
        out_shape=jax.ShapeDtypeStruct((nodes, width), BF16),
        in_specs=spaces,
        out_specs=any_,
        scratch_shapes=[pltpu.VMEM((nodes, width), BF16), pltpu.SemaphoreType.DMA((4,))],
        compiler_params=pltpu.CompilerParams(vmem_limit_bytes=40 * 2**20),
        cost_estimate=pl.CostEstimate(flops=6 * 10**8, bytes_accessed=2**20, transcendentals=10**3),
        name="last",
    )(*between)


def solution(mesh):
    split = ("gx", "gy")
    return jax.shard_map(
        body,
        mesh=mesh,
        in_specs=(
            P(split, None), P(split, None, None), P(split, None), P(split, None, None), P(split, None, None),
            P(split), P(), P(), P(), P(), P(), P(),
        ),
        out_specs=P(split, None),
        check_vma=False,
    )
```
